32 devices in a mesh: row: 2 (over y), col: 4 (over z), depth: 4 (over x, core).
Axes of the slice: x: 2, y: 2, z: 4, core: 2. Of those that a mesh axis runs over, the one named last changes fastest.
Arguments:
- a_blocks: bfloat16 [2, 4, 4, 16, 64, 256], P('row', 'col', 'depth'), may hold values from -0.5 to 0.5
- a_columns: int32 [2, 4, 4, 16, 4], P('row', 'col', 'depth'), may hold values from 0 to 127, as said below
- a_counts: int32 [2, 4, 4, 16], P('row', 'col', 'depth'), may hold values from 1 to 4, as said below
- b_blocks: bfloat16 [2, 4, 4, 128, 64, 128], P('row', 'col', 'depth'), may hold values from -6 to 6
- b_columns: int32 [2, 4, 4, 128, 2], P('row', 'col', 'depth'), may hold values from 0 to 191, as said below
- b_counts: int32 [2, 4, 4, 128], P('row', 'col', 'depth'), may hold values from 1 to 2, as said below
- c_columns: int32 [2, 4, 16, 4], P('row', 'col'), may hold values from 0 to 191, as said below
- c_counts: int32 [2, 4, 16], P('row', 'col'), may hold values from 1 to 4, as said below
Outputs:
- c_blocks: bfloat16 [2, 4, 16, 64, 256], P('row', 'col', 'depth')
The draws below stay inside these ranges and needn't reach their ends.
Inputs may be any that keep to these rules, and one draw needn't show every extreme that they name: `a_columns`: within one block row the listed inner blocks are distinct. `a_counts`: every A panel has a block row with 4 live slots. `b_columns`: within one block row the listed block columns are distinct. `b_counts`: the counts of every B panel sum to exactly 160. `c_columns`: within one block row the listed block columns are distinct. `c_counts`: every grid position has a block row with 4 live slots.
All inputs are finite; a program needn't handle non-finite values.
Results may differ from the reference program's by a relative error of at most 0.0065.
Values may be sent and summed in bfloat16 or wider, within the bound.
No kernel may reach another device: no remote copies, remote signals or barrier semaphores. Data moves between devices by JAX's collectives and lax.ppermute only.
A program may use at most 64 MiB of HBM per device.

```python
import jax
import jax.numpy as jnp
from jax import lax

BS = 64
BR = 16
BK = 128
BC = 192
KA = 4
JB = 2
JC = 4
STEPS = 2
N_ROW = 2
N_COL = 4
N_DEPTH = 4


def window_picks(key, row_total, picks, window, centers, modulus):
    all_keys = jax.random.split(key, row_total)
    offsets = jax.vmap(lambda one_key: jax.random.permutation(one_key, window)[:picks])(all_keys)
    return (centers[:, None] + offsets - window // 2) % modulus


def ragged_counts(key, tile_count, length, largest):
    first_key, second_key = jax.random.split(key)
    values = jax.random.randint(first_key, (tile_count, length), 1, largest + 1)
    full_row = jax.random.randint(second_key, (tile_count, 1), 0, length)
    return jnp.where(jnp.arange(length)[None, :] == full_row, largest, values).astype(jnp.int32)


def draw_a_columns(key, part):
    tile_count = N_ROW * N_COL * N_DEPTH
    row_pos = jnp.arange(tile_count * BR, dtype=jnp.int32) % BR
    centers = row_pos * BK // BR
    picked = window_picks(key, tile_count * BR, KA, 2 * KA, centers, BK)
    return picked.reshape(N_ROW, N_COL, N_DEPTH, BR, KA).astype(jnp.int32)


def draw_a_counts(key, part):
    counts = ragged_counts(key, N_ROW * N_COL * N_DEPTH, BR, KA)
    return counts.reshape(N_ROW, N_COL, N_DEPTH, BR)


def draw_b_columns(key, part):
    tile_count = N_ROW * N_COL * N_DEPTH
    row_pos = jnp.arange(tile_count * BK, dtype=jnp.int32) % BK
    centers = row_pos * BC // BK
    picked = window_picks(key, tile_count * BK, JB, 2 * JB, centers, BC)
    return picked.reshape(N_ROW, N_COL, N_DEPTH, BK, JB).astype(jnp.int32)


def draw_b_counts(key, part):
    tile_count = N_ROW * N_COL * N_DEPTH
    all_keys = jax.random.split(key, tile_count)
    ranks = jax.vmap(lambda one_key: jax.random.permutation(one_key, BK))(all_keys)
    counts = 1 + (JB - 1) * (ranks < BK // 4).astype(jnp.int32)
    return counts.reshape(N_ROW, N_COL, N_DEPTH, BK).astype(jnp.int32)


def draw_c_columns(key, part):
    tile_count = N_ROW * N_COL
    row_pos = jnp.arange(tile_count * BR, dtype=jnp.int32) % BR
    centers = row_pos * BK // BR * BC // BK
    picked = window_picks(key, tile_count * BR, JC, 4 * JC, centers, BC)
    return picked.reshape(N_ROW, N_COL, BR, JC).astype(jnp.int32)


def draw_c_counts(key, part):
    counts = ragged_counts(key, N_ROW * N_COL, BR, JC)
    return counts.reshape(N_ROW, N_COL, BR)


def block_levels(own_key, shape, pieces, low, high):
    gain = 1.0
    for dim, parts in pieces:
        heights = jax.random.uniform(jax.random.fold_in(jax.random.fold_in(own_key, 6), dim), (parts,), jnp.float32, low / len(pieces), high / len(pieces))
        gain = gain * jnp.repeat(jnp.exp(heights), shape[dim] // parts).reshape((-1,) + (1,) * (len(shape) - 1 - dim))
    return gain


def bell_draw(rng, shape, width, reach, cuts=(), held_as=jnp.bfloat16):
    array = width * jax.random.normal(rng, shape, jnp.float32)
    if cuts:
        array = array * block_levels(rng, shape, cuts, -0.22, 0.18)
    return jnp.clip(array, -reach, reach).astype(held_as)


def setup_inputs(seed: int = 0) -> dict:
    key_of = jax.random.split(jax.random.key(seed), 9)
    a_blocks = bell_draw(key_of[0], (N_ROW, N_COL, N_DEPTH, BR, BS, KA * BS), (2 * BS) ** -0.5, 0.5, ((0, 2), (1, 4), (2, 4)))
    a_columns = draw_a_columns(jax.random.fold_in(key_of[8], 71), 0)
    a_counts = draw_a_counts(jax.random.fold_in(key_of[8], 71), 0)
    b_blocks = bell_draw(key_of[3], (N_ROW, N_COL, N_DEPTH, BK, BS, JB * BS), 1.0, 6.0, ((0, 2), (1, 4), (2, 4)))
    b_columns = draw_b_columns(jax.random.fold_in(key_of[8], 71), 0)
    b_counts = draw_b_counts(jax.random.fold_in(key_of[8], 71), 0)
    c_columns = draw_c_columns(jax.random.fold_in(key_of[8], 71), 0)
    c_counts = draw_c_counts(jax.random.fold_in(key_of[8], 71), 0)
    return dict(a_blocks=a_blocks, a_columns=a_columns, a_counts=a_counts, b_blocks=b_blocks, b_columns=b_columns, b_counts=b_counts, c_columns=c_columns, c_counts=c_counts)


def block_product(a_panel, a_cols, a_live_counts, b_panel, b_cols, b_live_counts, c_cols, c_live_counts):
    row_count, block_size, a_width = a_panel.shape
    a_slots = a_cols.shape[1]
    b_slots = b_cols.shape[1]
    c_slots = c_cols.shape[1]
    a_split = a_panel.reshape(row_count, block_size, a_slots, block_size).astype(jnp.float32)
    b_rows = b_panel[a_cols].astype(jnp.float32)
    products = jnp.einsum("ipak,iakq->iapq", a_split, b_rows, precision=lax.Precision.HIGHEST)
    products = products.reshape(row_count, a_slots, block_size, b_slots, block_size)
    a_live = jnp.arange(a_slots, dtype=jnp.int32)[None, :] < a_live_counts[:, None]
    b_live = (jnp.arange(b_slots, dtype=jnp.int32)[None, :] < b_live_counts[:, None])[a_cols]
    b_target = b_cols[a_cols]
    c_live = jnp.arange(c_slots, dtype=jnp.int32)[None, :] < c_live_counts[:, None]
    matched = (b_target[:, :, :, None] == c_cols[:, None, None, :]) & a_live[:, :, None, None] & b_live[:, :, :, None] & c_live[:, None, None, :]
    summed = jnp.einsum("iapjq,iajm->ipmq", products, matched.astype(jnp.float32), precision=lax.Precision.HIGHEST)
    return summed.reshape(row_count, block_size, c_slots * block_size)


def reference(a_blocks, a_columns, a_counts, b_blocks, b_columns, b_counts, c_columns, c_counts):
    def one_tile(position):
        grid_row = position // N_COL
        grid_col = position % N_COL
        outcome = jnp.zeros((BR, BS, JC * BS), jnp.float32)
        for layer in range(N_DEPTH):
            partial_value = jnp.zeros((BR, BS, JC * BS), jnp.float32)
            for step in range(STEPS):
                a_row = (grid_row + step) % N_ROW
                b_col = (grid_col + step) % N_COL
                partial_value = partial_value + block_product(
                    a_blocks[a_row, grid_col, layer], a_columns[a_row, grid_col, layer], a_counts[a_row, grid_col, layer],
                    b_blocks[grid_row, b_col, layer], b_columns[grid_row, b_col, layer], b_counts[grid_row, b_col, layer],
                    c_columns[grid_row, grid_col], c_counts[grid_row, grid_col])
            rounded = lax.optimization_barrier(partial_value.astype(jnp.bfloat16))
            outcome = outcome + rounded.astype(jnp.float32)
        return outcome.astype(jnp.bfloat16)

    tiles = lax.map(one_tile, jnp.arange(N_ROW * N_COL, dtype=jnp.int32))
    return tiles.reshape(N_ROW, N_COL, BR, BS, JC * BS)
```

```python
import functools

import jax
import jax.numpy as jnp
from jax import lax
from jax.experimental import pallas as pl
from jax.experimental.pallas import tpu as pltpu
from jax.sharding import PartitionSpec as P

SMEM = pltpu.SMEM
VMEM = pltpu.VMEM


def select_row(i, b_ref, lists, sel_ref):
    a_col, a_cnt, b_col, b_cnt, c_col, c_cnt = lists
    block, width = b_ref.shape[1:]
    a_slots, c_slots = a_col.shape[0], c_col.shape[0]
    left = lax.broadcasted_iota(jnp.int32, (1, width), 1) < block
    target = [jnp.where(m < c_cnt[0, i], c_col[m, i], -1) for m in range(c_slots)]
    pairs = [jnp.where(left, target[m], target[m + 1]) for m in range(0, c_slots, 2)]
    for a in range(a_slots):
        k = a_col[a, i]
        live = jnp.where(a < a_cnt[0, i], b_cnt[0, k], 0)
        first = jnp.where(0 < live, b_col[0, k], -2)
        second = jnp.where(1 < live, b_col[1, k], -2)
        straight = jnp.where(left, first, second)
        crossed = jnp.where(left, second, first)
        rows = b_ref[k]
        swapped = jnp.concatenate([rows[:, block:], rows[:, :block]], axis=1)
        for p, wanted in enumerate(pairs):
            keep = (straight == wanted).astype(jnp.float32).astype(rows.dtype)
            swap = (crossed == wanted).astype(jnp.float32).astype(rows.dtype)
            sel_ref[a * block : (a + 1) * block, p * width : (p + 1) * width] = rows * keep + swapped * swap


def chunk_rows(total, parts):
    return total // parts


def own_kernel(parts, a_ref, b_ref, a_col, a_cnt, b_col, b_cnt, c_col, c_cnt, *rest):
    outs, sel = rest[:parts], rest[parts]
    lists = (a_col, a_cnt, b_col, b_cnt, c_col, c_cnt)
    me = lax.axis_index("depth")
    rows = a_ref.shape[0] // parts
    for n in range(parts):
        base = (me ^ n) * rows

        def body(j, carry, n=n, base=base):
            i = base + j
            select_row(i, b_ref, lists, sel.at[j % 2])
            got = jnp.dot(a_ref[i], sel[j % 2], preferred_element_type=jnp.float32)
            outs[n][j] = got.astype(outs[n].dtype)
            return carry

        lax.fori_loop(0, rows, body, 0, unroll=2)


def select_kernel(parts, b_ref, a_col, a_cnt, b_col, b_cnt, c_col, c_cnt, *outs):
    lists = (a_col, a_cnt, b_col, b_cnt, c_col, c_cnt)
    me = lax.axis_index("depth")
    rows = outs[0].shape[0]
    for n in range(parts):
        base = (me ^ n) * rows

        def body(j, carry, n=n, base=base):
            select_row(base + j, b_ref, lists, outs[n].at[j])
            return carry

        lax.fori_loop(0, rows, body, 0, unroll=2)


def far_kernel(order, a_ref, *refs):
    count = len(order)
    sels, outs = refs[:count], refs[count:]
    me = lax.axis_index("depth")
    rows = a_ref.shape[0] // count
    for sel, out, n in zip(sels, outs, order):
        base = ((me ^ n) % count) * rows
        for j in range(rows):
            got = jnp.dot(a_ref[base + j], sel[j], preferred_element_type=jnp.float32)
            out[j] = got.astype(out.dtype)


def sent(value, sizes, shift_row, shift_col, flip_depth):
    rows, cols, layers = sizes
    pairs = []
    for r in range(rows):
        for c in range(cols):
            for l in range(layers):
                here = (r * cols + c) * layers + l
                there = (((r + shift_row) % rows) * cols + (c + shift_col) % cols) * layers + (l ^ flip_depth)
                pairs.append((here, there))
    return lax.ppermute(value, ("row", "col", "depth"), pairs)


def local(sizes, a_blocks, a_columns, a_counts, b_blocks, b_columns, b_counts, c_columns, c_counts):
    layers = sizes[2]
    a = a_blocks[0, 0, 0]
    b = b_blocks[0, 0, 0]
    a_col, a_cnt = a_columns[0, 0, 0].T, a_counts[0, 0]
    b_col, b_cnt = b_columns[0, 0, 0].T, b_counts[0, 0]
    c_col, c_cnt = c_columns[0, 0].T, c_counts[0]
    total, block, width = a.shape
    rows = total // layers
    half = layers // 2
    out_width = c_col.shape[0] * block
    me = lax.axis_index("depth")
    spec = lambda space: pl.BlockSpec(memory_space=space)
    piece = jax.ShapeDtypeStruct((rows, block, out_width), a.dtype)

    far_a = []
    for side in (1, 0):
        start = ((me // half) ^ side) * (half * rows)
        part = lax.dynamic_slice_in_dim(a, start, half * rows, 0)
        far_a.append(sent(part, sizes, -1, 1, 0))
    far_a_col = sent(a_col, sizes, -1, 1, 0)
    far_a_cnt = sent(a_cnt, sizes, -1, 1, 0)
    far_c_col = sent(c_col, sizes, 0, 1, 0)
    far_c_cnt = sent(c_cnt, sizes, 0, 1, 0)

    own = pl.pallas_call(
        functools.partial(own_kernel, layers),
        out_shape=[piece] * layers,
        in_specs=[spec(VMEM)] * 2 + [spec(SMEM)] * 6,
        out_specs=[spec(VMEM)] * layers,
        scratch_shapes=[VMEM((2, width, out_width), a.dtype)],
        cost_estimate=pl.CostEstimate(flops=2 * total * block * width * out_width, bytes_accessed=4 << 20, transcendentals=0),
        name="own_product",
    )(a, b, a_col, a_cnt, b_col, b_cnt, c_col, c_cnt)
    pieces = [own[0]] + [sent(own[n], sizes, 0, 0, n) for n in range(1, layers)]

    chosen = pl.pallas_call(
        functools.partial(select_kernel, layers),
        out_shape=[jax.ShapeDtypeStruct((rows, width, out_width), a.dtype)] * layers,
        in_specs=[spec(VMEM)] + [spec(SMEM)] * 6,
        out_specs=[spec(VMEM)] * layers,
        cost_estimate=pl.CostEstimate(flops=0, bytes_accessed=4 << 20, transcendentals=0),
        name="far_select",
    )(b, far_a_col, far_a_cnt, b_col, b_cnt, far_c_col, far_c_cnt)
    for side, part in zip((1, 0), far_a):
        order = tuple(range(side * half, (side + 1) * half))
        got = pl.pallas_call(
            functools.partial(far_kernel, order),
            out_shape=[piece] * half,
            in_specs=[spec(VMEM)] * (1 + half),
            out_specs=[spec(VMEM)] * half,
            cost_estimate=pl.CostEstimate(flops=total * block * width * out_width, bytes_accessed=2 << 20, transcendentals=0),
            name="far_product",
        )(part, *[chosen[n] for n in order])
        pieces += [sent(one, sizes, 0, -1, n) for one, n in zip(got, order)]
    outcome = sum(one.astype(jnp.float32) for one in pieces)
    return outcome.astype(a.dtype)[None, None]


def solution(mesh):
    placed = (
        P("row", "col", "depth", None, None, None),
        P("row", "col", "depth", None, None),
        P("row", "col", "depth", None),
        P("row", "col", "depth", None, None, None),
        P("row", "col", "depth", None, None),
        P("row", "col", "depth", None),
        P("row", "col", None, None),
        P("row", "col", None),
    )
    sizes = (mesh.shape["row"], mesh.shape["col"], mesh.shape["depth"])
    return jax.shard_map(
        functools.partial(local, sizes),
        mesh=mesh,
        in_specs=placed,
        out_specs=P("row", "col", "depth", None, None),
        check_vma=False,
    )
```

```python
import functools

import jax
import jax.numpy as jnp
from jax import lax
from jax.experimental import pallas as pl
from jax.experimental.pallas import tpu as pltpu
from jax.sharding import PartitionSpec as P

ANY = pl.BlockSpec(memory_space=pl.ANY)
AXES = ("row", "col", "depth")


def select_row(i, b_ref, a_list, c_list, b_col, b_cnt, shape, sel_ref):
    a_slots, c_slots = shape
    block, width = b_ref.shape[1:]
    left = lax.broadcasted_iota(jnp.int32, (1, width), 1) < block
    target = [c_list[a_slots + m, i] for m in range(c_slots)]
    pairs = [jnp.where(left, target[m], target[m + 1]) for m in range(0, c_slots, 2)]
    for a in range(a_slots):
        listed = a_list[a, i]
        k = jnp.maximum(listed, 0)
        live = jnp.where(listed < 0, 0, b_cnt[0, k])
        first = jnp.where(0 < live, b_col[0, k], -2)
        second = jnp.where(1 < live, b_col[1, k], -2)
        straight = jnp.where(left, first, second)
        crossed = jnp.where(left, second, first)
        rows = b_ref[k]
        swapped = jnp.concatenate([rows[:, block:], rows[:, :block]], axis=1)
        for p, wanted in enumerate(pairs):
            keep = (straight == wanted).astype(jnp.float32).astype(rows.dtype)
            swap = (crossed == wanted).astype(jnp.float32).astype(rows.dtype)
            sel_ref[a * block : (a + 1) * block, p * width : (p + 1) * width] = rows * keep + swapped * swap


def product_kernel(shape, order, count, a_hbm, b_hbm, a_list_hbm, c_list_hbm, b_col_hbm, b_cnt_hbm, *rest):
    outs, (a_ref, b_ref, a_list, c_list, b_col, b_cnt, sel, sems) = rest[: len(order)], rest[len(order) :]
    pairs = ((a_list_hbm, a_list), (c_list_hbm, c_list), (b_col_hbm, b_col), (b_cnt_hbm, b_cnt), (a_hbm, a_ref), (b_hbm, b_ref))
    copies = [pltpu.make_async_copy(source, target, sems.at[at]) for at, (source, target) in enumerate(pairs)]
    for copy in copies:
        copy.start()
    me = lax.axis_index("depth")
    rows = a_ref.shape[0] // count
    for copy in copies:
        copy.wait()
    for n, out in zip(order, outs):
        slot = me ^ n
        first = slot * rows
        here = (slot % count) * rows
        for j in range(rows):
            select_row(first + j, b_ref, a_list, c_list, b_col, b_cnt, shape, sel.at[j])
        for j in range(rows):
            got = jnp.dot(a_ref[here + j], sel[j], preferred_element_type=jnp.float32)
            out[j] = got.astype(out.dtype)


def product(shape, order, count, a, b, a_list, c_list, b_col, b_cnt, name):
    total, block, width = a.shape
    rows = total // count
    out_width = shape[1] * block
    piece = jax.ShapeDtypeStruct((rows, block, out_width), a.dtype)
    operands = (a, b, a_list, c_list, b_col, b_cnt)
    smem = [pltpu.SMEM(x.shape, x.dtype) for x in operands[2:]]
    return pl.pallas_call(
        functools.partial(product_kernel, shape, order, count),
        out_shape=[piece] * len(order),
        in_specs=[ANY] * len(operands),
        out_specs=[pl.BlockSpec(memory_space=pltpu.VMEM)] * len(order),
        scratch_shapes=[pltpu.VMEM(a.shape, a.dtype), pltpu.VMEM(b.shape, b.dtype), *smem]
        + [pltpu.VMEM((rows, width, out_width), a.dtype), pltpu.SemaphoreType.DMA((len(operands),))],
        compiler_params=pltpu.CompilerParams(vmem_limit_bytes=16 << 20),
        cost_estimate=pl.CostEstimate(flops=2 * total * block * width * out_width, bytes_accessed=4 << 20, transcendentals=0),
        name=name,
    )(*operands)


def sent(value, sizes, shift_row, shift_col, flip_depth):
    rows, cols, layers = sizes
    pairs = []
    for r in range(rows):
        for c in range(cols):
            for l in range(layers):
                here = (r * cols + c) * layers + l
                there = (((r + shift_row) % rows) * cols + (c + shift_col) % cols) * layers + (l ^ flip_depth)
                pairs.append((here, there))
    return lax.ppermute(value, AXES, pairs)


def live_columns(columns, counts):
    slots = columns.shape[1]
    return jnp.where(jnp.arange(slots, dtype=jnp.int32)[:, None] < counts[None, :], columns.T, -1)


def local(sizes, a_blocks, a_columns, a_counts, b_blocks, b_columns, b_counts, c_columns, c_counts):
    layers = sizes[2]
    half = layers // 2
    a, b = a_blocks[0, 0, 0], b_blocks[0, 0, 0]
    b_col, b_cnt = b_columns[0, 0, 0].T, b_counts[0, 0]
    rows = a.shape[0] // layers
    shape = (a_columns.shape[-1], c_columns.shape[-1])
    me = lax.axis_index("depth")

    lists = jnp.concatenate([live_columns(a_columns[0, 0, 0], a_counts[0, 0, 0]), live_columns(c_columns[0, 0], c_counts[0, 0])])
    a_later, lists = lax.optimization_barrier((a, lists))
    far_a = []
    for side, source in ((1, a), (0, a_later)):
        start = ((me // half) ^ side) * (half * rows)
        part = lax.dynamic_slice_in_dim(source, start, half * rows, 0)
        far_a.append(sent(part, sizes, -1, 1, 0))
    far_a_list = sent(lists, sizes, -1, 1, 0)
    far_c_list = sent(lists, sizes, 0, 1, 0)

    own = product(shape, tuple(range(layers)), layers, a, b, lists, lists, b_col, b_cnt, "own_product")
    own, far_a_list, far_c_list = lax.optimization_barrier((own, far_a_list, far_c_list))
    pieces = [own[0]] + [sent(own[n], sizes, 0, 0, n) for n in range(1, layers)]
    for side, part in zip((1, 0), far_a):
        order = tuple(range(side * half, (side + 1) * half))
        if side == 0:
            part, got = lax.optimization_barrier((part, got))
            pieces[-half:] = [sent(one, sizes, 0, -1, n) for one, n in zip(got, range(half, layers))]
        got = product(shape, order, half, part, b, far_a_list, far_c_list, b_col, b_cnt, "far_product")
        pieces += [sent(one, sizes, 0, -1, n) for one, n in zip(got, order)]
    outcome = sum(one.astype(jnp.float32) for one in pieces)
    return outcome.astype(a.dtype)[None, None]


def solution(mesh):
    placed = (
        P("row", "col", "depth", None, None, None),
        P("row", "col", "depth", None, None),
        P("row", "col", "depth", None),
        P("row", "col", "depth", None, None, None),
        P("row", "col", "depth", None, None),
        P("row", "col", "depth", None),
        P("row", "col", None, None),
        P("row", "col", None),
    )
    sizes = tuple(mesh.shape[axis] for axis in AXES)
    return jax.shard_map(
        functools.partial(local, sizes),
        mesh=mesh,
        in_specs=placed,
        out_specs=P("row", "col", "depth", None, None),
        check_vma=False,
    )
```

```python
import functools

import jax
import jax.numpy as jnp
from jax import lax
from jax.experimental import pallas as pl
from jax.experimental.pallas import tpu as pltpu
from jax.sharding import PartitionSpec as P

ANY = pl.BlockSpec(memory_space=pl.ANY)
HBM = pl.BlockSpec(memory_space=pltpu.HBM)
VMEM = pl.BlockSpec(memory_space=pltpu.VMEM)
DEAD_B, DEAD_C = -2, -1
OWN = 2
FAR = 100
AXES = ("row", "col", "depth")


def fill_b_list(b_list, b_col, b_cnt, block):
    slots, inner = b_col.shape
    width = b_list.shape[1]
    number = lax.broadcasted_iota(jnp.int32, (slots, inner), 0)
    live = jnp.where(number < b_cnt[...], b_col[...], DEAD_B)
    live = jnp.concatenate([live, jnp.full((8 - slots, inner), DEAD_B, jnp.int32)]).T
    first, second = (jnp.broadcast_to(live[:, slot : slot + 1], (inner, width)) for slot in range(2))
    left = lax.broadcasted_iota(jnp.int32, (inner, width), 1) < block
    half = b_list.shape[0] // 2
    b_list[:inner, :] = jnp.where(left, first, second)
    b_list[half : half + inner, :] = jnp.where(left, second, first)
    for start in (inner, half + inner):
        b_list[start : start + half - inner, :] = jnp.full((half - inner, width), DEAD_B, jnp.int32)


def select_row(i, b_ref, lists, b_list, sel_ref):
    inner, block, width = b_ref.shape
    a_slots, c_slots = sel_ref.shape[0] // block, sel_ref.shape[1] // block
    left = lax.broadcasted_iota(jnp.int32, (1, width), 1) < block
    listed = pltpu.roll(lists[...], lists.shape[1] - i, 1)
    target = [listed[a_slots + m, 0] for m in range(c_slots)]
    pairs = [jnp.where(left, target[m], target[m + 1]) for m in range(0, c_slots, 2)]
    for a in range(a_slots):
        k = listed[a, 0]
        straight = b_list[pl.ds(k, 1), :]
        crossed = b_list[pl.ds(k + b_list.shape[0] // 2, 1), :]
        rows = b_ref[jnp.minimum(k, inner - 1)]
        swapped = jnp.concatenate([rows[:, block:], rows[:, :block]], axis=1)
        for p, wanted in enumerate(pairs):
            keep = (straight == wanted).astype(jnp.float32).astype(rows.dtype)
            swap = (crossed == wanted).astype(jnp.float32).astype(rows.dtype)
            sel_ref[a * block : (a + 1) * block, p * width : (p + 1) * width] = rows * keep + swapped * swap


def product_kernel(groups, fills, *refs):
    a_ref, b_ref, a_list, c_list = refs[:4]
    if fills:
        b_col, b_cnt = refs[4:6]
        *outs, b_list, lists, sel = refs[6:]
        fill_b_list(b_list, b_col, b_cnt, b_ref.shape[1])
    else:
        b_list, *outs, lists, sel = refs[4:]
    a_slots, listed = a_list.shape
    lists[:a_slots, :listed] = a_list[...]
    lists[a_slots : a_slots + c_list.shape[0], :listed] = c_list[...]
    me = lax.axis_index("depth")
    rows = sel.shape[0]
    for group, out in zip(groups, outs):
        for at, n in enumerate(group):
            first = (me ^ n) * rows
            for j in range(rows):
                select_row(first + j, b_ref, lists, b_list, sel.at[j])
            for j in range(rows):
                got = jnp.dot(a_ref[first + j], sel[j], preferred_element_type=jnp.float32)
                out[at * rows + j] = got.astype(out.dtype)


def product(layers, groups, a, b, a_list, c_list, b_lists, name, limit, weight):
    total, block, width = a.shape
    inner, _, b_width = b.shape
    rows = total // layers
    out_width = c_list.shape[0] * block
    fills = len(b_lists) == 2
    outs = [jax.ShapeDtypeStruct((len(group) * rows, block, out_width), a.dtype) for group in groups]
    if fills:
        outs.append(jax.ShapeDtypeStruct((2 * (inner + 8), b_width), jnp.int32))
    return pl.pallas_call(
        functools.partial(product_kernel, groups, fills),
        out_shape=outs,
        in_specs=[VMEM] * (4 + len(b_lists)),
        out_specs=[VMEM] * len(outs),
        scratch_shapes=[pltpu.VMEM((8, 128), jnp.int32), pltpu.VMEM((rows, width, out_width), a.dtype)],
        compiler_params=pltpu.CompilerParams(vmem_limit_bytes=limit),
        cost_estimate=pl.CostEstimate(flops=weight * total * block * width * out_width, bytes_accessed=0, transcendentals=0),
        name=name,
    )(a, b, a_list, c_list, *b_lists)


def total_of(pieces, dtype):
    return sum(one.astype(jnp.float32) for one in pieces).astype(dtype)


def sent(value, sizes, shift_row, shift_col, flip_depth):
    rows, cols, layers = sizes
    shifts = [move if isinstance(move, tuple) else (move, move) for move in (shift_row, shift_col, flip_depth)]
    pairs = []
    for r in range(rows):
        for c in range(cols):
            for l in range(layers):
                by_row, by_col, flip = (move[l % 2] for move in shifts)
                here = (r * cols + c) * layers + l
                there = (((r + by_row) % rows) * cols + (c + by_col) % cols) * layers + (l ^ flip)
                pairs.append((here, there))
    return lax.ppermute(value, AXES, pairs)


def live_columns(columns, counts, dead):
    return jnp.where(jnp.arange(columns.shape[1], dtype=jnp.int32)[:, None] < counts[None, :], columns.T, dead)


def local(sizes, a_blocks, a_columns, a_counts, b_blocks, b_columns, b_counts, c_columns, c_counts):
    layers = sizes[2]
    a, b = a_blocks[0, 0, 0], b_blocks[0, 0, 0]
    rows = a.shape[0] // layers
    evens, odds = tuple(range(0, layers, 2)), tuple(range(1, layers, 2))

    far_a = sent(a, sizes, -1, 1, 0)
    a_list = live_columns(a_columns[0, 0, 0], a_counts[0, 0, 0], b.shape[0])
    c_list = live_columns(c_columns[0, 0], c_counts[0, 0], DEAD_C)
    far_a_list = sent(a_list, sizes, -1, 1, 0)
    far_c_list = sent(c_list, sizes, 0, 1, 0)

    def paired(passed, kept):
        met = sent(passed, sizes, 0, 0, 1)
        return [total_of((one, met[at * rows : (at + 1) * rows]), a.dtype) for at, one in enumerate(kept)]

    singles = tuple((n,) for n in evens)
    raw = (b_columns[0, 0, 0].T, b_counts[0, 0])
    passed, *kept, b_list = product(layers, (odds,) + singles, a, b, a_list, c_list, raw, "own_product", 8 << 20, OWN)
    own = paired(passed, kept)
    far_a, own = lax.optimization_barrier((far_a, own))
    (passed,) = product(layers, (odds,), far_a, b, far_a_list, far_c_list, (b_list,), "far_passed", 8 << 20, FAR)
    far_a, passed = lax.optimization_barrier((far_a, passed))
    kept = product(layers, singles, far_a, b, far_a_list, far_c_list, (b_list,), "far_kept", 8 << 20, FAR)
    far = paired(passed, kept)
    even = lax.axis_index("depth") % 2 == 0
    pieces = [own[0]]
    for own_piece, own_n, far_piece, far_n in zip(own[1:], evens[1:], far, evens):
        for own_side in (0, 1):
            moves = ((0, 0, own_n), (0, -1, far_n)) if own_side == 0 else ((0, -1, far_n), (0, 0, own_n))
            mixed = jnp.where(even == (own_side == 0), own_piece, far_piece)
            pieces.append(sent(mixed, sizes, *zip(*moves)))
    pieces.append(sent(far[-1], sizes, 0, -1, evens[-1]))
    return total_of(pieces, a.dtype)[None, None]


def solution(mesh):
    placed = (
        P("row", "col", "depth", None, None, None),
        P("row", "col", "depth", None, None),
        P("row", "col", "depth", None),
        P("row", "col", "depth", None, None, None),
        P("row", "col", "depth", None, None),
        P("row", "col", "depth", None),
        P("row", "col", None, None),
        P("row", "col", None),
    )
    sizes = tuple(mesh.shape[axis] for axis in AXES)
    return jax.shard_map(
        functools.partial(local, sizes),
        mesh=mesh,
        in_specs=placed,
        out_specs=P("row", "col", "depth", None, None),
        check_vma=False,
    )
```

```python
import functools

import jax
import jax.numpy as jnp
from jax import lax
from jax.experimental import pallas as pl
from jax.experimental.pallas import tpu as pltpu
from jax.sharding import PartitionSpec as P

ANY = pl.BlockSpec(memory_space=pl.ANY)
HBM = pl.BlockSpec(memory_space=pltpu.HBM)
VMEM = pl.BlockSpec(memory_space=pltpu.VMEM)
DEAD_B = -1
OWN = 2
SLICE = 10000
FAR = 100
AXES = ("row", "col", "depth")


def fill_b_list(b_list, live, block):
    slots, inner = live.shape
    width = b_list.shape[1]
    columns = jnp.concatenate([live[...], jnp.full((8 - slots, inner), DEAD_B, jnp.int32)]).T
    first, second = (jnp.broadcast_to(columns[:, slot : slot + 1], (inner, width)) for slot in range(2))
    left = lax.broadcasted_iota(jnp.int32, (inner, width), 1) < block
    half = b_list.shape[0] // 2
    b_list[:inner, :] = jnp.where(left, first, second)
    b_list[half : half + inner, :] = jnp.where(left, second, first)
    for start in (inner, half + inner):
        b_list[start : start + half - inner, :] = jnp.full((half - inner, width), DEAD_B, jnp.int32)


def select_row(i, b_ref, lists, b_list, sel_ref):
    inner, block, width = b_ref.shape
    a_slots, c_slots = sel_ref.shape[0] // block, sel_ref.shape[1] // block
    left = lax.broadcasted_iota(jnp.int32, (1, width), 1) < block
    listed = pltpu.roll(lists[...], lists.shape[1] - i, 1)
    target = [listed[a_slots + m, 0] for m in range(c_slots)]
    pairs = [jnp.where(left, target[m], target[m + 1]) for m in range(0, c_slots, 2)]
    for a in range(a_slots):
        k = listed[a, 0]
        straight = b_list[pl.ds(k, 1), :]
        crossed = b_list[pl.ds(k + b_list.shape[0] // 2, 1), :]
        rows = b_ref[jnp.minimum(k, inner - 1)]
        swapped = jnp.concatenate([rows[:, block:], rows[:, :block]], axis=1)
        for p, wanted in enumerate(pairs):
            keep = (straight == wanted).astype(jnp.float32).astype(rows.dtype)
            swap = (crossed == wanted).astype(jnp.float32).astype(rows.dtype)
            sel_ref[a * block : (a + 1) * block, p * width : (p + 1) * width] = rows * keep + swapped * swap


def product_kernel(groups, count, fills, *refs):
    a_ref, b_ref, a_list, c_list, b_list, *outs, lists, sel = refs
    if fills:
        live, b_list = b_list, outs.pop()
        fill_b_list(b_list, live, b_ref.shape[1])
    a_slots, listed = a_list.shape
    lists[:a_slots, :listed] = a_list[...]
    lists[a_slots : a_slots + c_list.shape[0], :listed] = c_list[...]
    me = lax.axis_index("depth")
    rows = sel.shape[0]
    for group, out in zip(groups, outs):
        for at, n in enumerate(group):
            slot = me ^ n
            first, here = slot * rows, slot % count * rows
            for j in range(rows):
                select_row(first + j, b_ref, lists, b_list, sel.at[j])
            for j in range(rows):
                got = jnp.dot(a_ref[here + j], sel[j], preferred_element_type=jnp.float32)
                out[at * rows + j] = got.astype(out.dtype)


def product(count, groups, a, b, a_list, c_list, b_list, name, weight):
    total, block, width = a.shape
    inner, _, b_width = b.shape
    rows = total // count
    out_width = c_list.shape[0] * block
    fills = b_list.shape[0] < inner
    outs = [jax.ShapeDtypeStruct((len(group) * rows, block, out_width), a.dtype) for group in groups]
    if fills:
        outs.append(jax.ShapeDtypeStruct((2 * (inner + 8), b_width), jnp.int32))
    return pl.pallas_call(
        functools.partial(product_kernel, groups, count, fills),
        out_shape=outs,
        in_specs=[VMEM] * 5,
        out_specs=[VMEM] * len(outs),
        scratch_shapes=[pltpu.VMEM((8, 128), jnp.int32), pltpu.VMEM((rows, width, out_width), a.dtype)],
        compiler_params=pltpu.CompilerParams(vmem_limit_bytes=8 << 20),
        cost_estimate=pl.CostEstimate(flops=weight * total * block * width * out_width, bytes_accessed=0, transcendentals=0),
        name=name,
    )(a, b, a_list, c_list, b_list)


def slice_kernel(parts, a_ref, out):
    out[...] = a_ref[pl.ds(lax.axis_index("depth") // (parts // 2) * out.shape[0], out.shape[0])]


def near_half(a, parts):
    return pl.pallas_call(
        functools.partial(slice_kernel, parts),
        out_shape=jax.ShapeDtypeStruct((a.shape[0] // 2, *a.shape[1:]), a.dtype),
        in_specs=[VMEM],
        out_specs=VMEM,
        compiler_params=pltpu.CompilerParams(vmem_limit_bytes=8 << 20),
        cost_estimate=pl.CostEstimate(flops=SLICE * a.size, bytes_accessed=0, transcendentals=0),
        name="near_half",
    )(a)


def total_of(pieces, dtype):
    return sum(one.astype(jnp.float32) for one in pieces).astype(dtype)


def sent(value, sizes, shift_row, shift_col, flip_depth):
    rows, cols, layers = sizes
    shifts = [move if isinstance(move, tuple) else (move, move) for move in (shift_row, shift_col, flip_depth)]
    pairs = []
    for r in range(rows):
        for c in range(cols):
            for l in range(layers):
                by_row, by_col, flip = (move[l % 2] for move in shifts)
                here = (r * cols + c) * layers + l
                there = (((r + by_row) % rows) * cols + (c + by_col) % cols) * layers + (l ^ flip)
                pairs.append((here, there))
    return lax.ppermute(value, AXES, pairs)


def live_columns(columns, counts, dead):
    return jnp.where(jnp.arange(columns.shape[1], dtype=jnp.int32)[:, None] < counts[None, :], columns.T, dead)


def local(sizes, a_blocks, a_columns, a_counts, b_blocks, b_columns, b_counts, c_columns, c_counts):
    layers = sizes[2]
    a, b = a_blocks[0, 0, 0], b_blocks[0, 0, 0]
    rows = a.shape[0] // layers
    evens, odds = tuple(range(0, layers, 2)), tuple(range(1, layers, 2))

    half = layers // 2
    side = lax.axis_index("depth") // half
    first = lax.dynamic_slice_in_dim(a, (1 - side) * (half * rows), half * rows, 0)
    far_first = sent(first, sizes, -1, 1, 0)
    first, a_counts, c_list = lax.optimization_barrier((first, a_counts, c_columns[0, 0].T))
    a_list = live_columns(a_columns[0, 0, 0], a_counts[0, 0, 0], b.shape[0])
    far_a_list = sent(a_list, sizes, -1, 1, 0)
    far_c_list = sent(c_list, sizes, 0, 1, 0)
    a_later, a_list = lax.optimization_barrier((a, a_list))
    far_second = sent(near_half(a_later, layers), sizes, -1, 1, 0)

    def paired(passed, kept):
        met = sent(passed, sizes, 0, 0, 1)
        return [total_of((one, met[at * rows : (at + 1) * rows]), a.dtype) for at, one in enumerate(kept)]

    def far_product(part, order, b_list):
        order_odds, order_evens = tuple(n for n in order if n % 2), tuple((n,) for n in order if n % 2 == 0)
        passed, *filled = product(half, (order_odds,), part, b, far_a_list, far_c_list, b_list, "far_passed", FAR)
        b_list = filled[0] if filled else b_list
        part, passed = lax.optimization_barrier((part, passed))
        kept = product(half, order_evens, part, b, far_a_list, far_c_list, b_list, "far_kept", FAR)
        return paired(passed, kept), b_list

    b_list = live_columns(b_columns[0, 0, 0], b_counts[0, 0, 0], DEAD_B)
    far, b_list = far_product(far_first, range(half, layers), b_list)
    a_later, far = lax.optimization_barrier((a_later, far))
    passed, *kept = product(layers, (odds,) + tuple((n,) for n in evens), a_later, b, a_list, c_list, b_list, "own_product", OWN)
    far_second, passed = lax.optimization_barrier((far_second, passed))
    own = paired(passed, kept)
    far = far_product(far_second, range(half), b_list)[0] + far
    even = lax.axis_index("depth") % 2 == 0
    pieces = [own[0]] + [sent(one, sizes, 0, -1, n) for one, n in zip(far[len(evens) // 2 :], evens[len(evens) // 2 :])]
    for own_piece, own_n, far_piece, far_n in zip(own[1:], evens[1:], far, evens):
        for own_side in (0, 1):
            moves = ((0, 0, own_n), (0, -1, far_n)) if own_side == 0 else ((0, -1, far_n), (0, 0, own_n))
            mixed = jnp.where(even == (own_side == 0), own_piece, far_piece)
            pieces.append(sent(mixed, sizes, *zip(*moves)))
    counts = lax.dynamic_slice_in_dim(c_counts[0, 0], lax.axis_index("depth") * rows, rows, 0)
    slot = jnp.arange(c_list.shape[0] * b.shape[1], dtype=jnp.int32) // b.shape[1]
    live = slot[None, None, :] < counts[:, None, None]
    return jnp.where(live, total_of(pieces, jnp.float32), 0).astype(a.dtype)[None, None]


def solution(mesh):
    placed = (
        P("row", "col", "depth", None, None, None),
        P("row", "col", "depth", None, None),
        P("row", "col", "depth", None),
        P("row", "col", "depth", None, None, None),
        P("row", "col", "depth", None, None),
        P("row", "col", "depth", None),
        P("row", "col", None, None),
        P("row", "col", None),
    )
    sizes = tuple(mesh.shape[axis] for axis in AXES)
    return jax.shard_map(
        functools.partial(local, sizes),
        mesh=mesh,
        in_specs=placed,
        out_specs=P("row", "col", "depth", None, None),
        check_vma=False,
    )
```

```python
import functools

import jax
import jax.numpy as jnp
from jax import lax
from jax.experimental import pallas as pl
from jax.experimental.pallas import tpu as pltpu
from jax.sharding import PartitionSpec as P

ANY = pl.BlockSpec(memory_space=pl.ANY)
HBM = pl.BlockSpec(memory_space=pltpu.HBM)
VMEM = pl.BlockSpec(memory_space=pltpu.VMEM)
DEAD_B = -1
OWN = 2
GATE = 5 << 30
TURN = 5 << 30
LIMIT = 8 << 20
FAR = 100
AXES = ("row", "col", "depth")


def fill_b_list(b_list, live, block):
    slots, inner = live.shape
    width = b_list.shape[1]
    columns = jnp.concatenate([live[...], jnp.full((8 - slots, inner), DEAD_B, jnp.int32)]).T
    first, second = (jnp.broadcast_to(columns[:, slot : slot + 1], (inner, width)) for slot in range(2))
    left = lax.broadcasted_iota(jnp.int32, (inner, width), 1) < block
    half = b_list.shape[0] // 2
    b_list[:inner, :] = jnp.where(left, first, second)
    b_list[half : half + inner, :] = jnp.where(left, second, first)
    for start in (inner, half + inner):
        b_list[start : start + half - inner, :] = jnp.full((half - inner, width), DEAD_B, jnp.int32)


def select_row(i, b_ref, lists, b_list, sel_ref):
    inner, block, width = b_ref.shape
    a_slots, c_slots = sel_ref.shape[0] // block, sel_ref.shape[1] // block
    left = lax.broadcasted_iota(jnp.int32, (1, width), 1) < block
    listed = pltpu.roll(lists[...], lists.shape[1] - i, 1)
    target = [listed[a_slots + m, 0] for m in range(c_slots)]
    pairs = [jnp.where(left, target[m], target[m + 1]) for m in range(0, c_slots, 2)]
    for a in range(a_slots):
        k = listed[a, 0]
        straight = b_list[pl.ds(k, 1), :]
        crossed = b_list[pl.ds(k + b_list.shape[0] // 2, 1), :]
        rows = b_ref[jnp.minimum(k, inner - 1)]
        swapped = jnp.concatenate([rows[:, block:], rows[:, :block]], axis=1)
        for p, wanted in enumerate(pairs):
            keep = (straight == wanted).astype(jnp.float32).astype(rows.dtype)
            swap = (crossed == wanted).astype(jnp.float32).astype(rows.dtype)
            sel_ref[a * block : (a + 1) * block, p * width : (p + 1) * width] = rows * keep + swapped * swap


def product_kernel(groups, count, fills, *refs):
    a_ref, b_ref, a_list, c_list, b_list, *outs, lists, sel = refs
    if fills:
        live, b_list = b_list, outs.pop()
        fill_b_list(b_list, live, b_ref.shape[1])
    a_slots, listed = a_list.shape
    lists[:a_slots, :listed] = a_list[...]
    lists[a_slots : a_slots + c_list.shape[0], :listed] = c_list[...]
    me = lax.axis_index("depth")
    rows = sel.shape[0]
    for group, out in zip(groups, outs):
        for at, n in enumerate(group):
            slot = me ^ n
            first, here = slot * rows, slot % count * rows
            for j in range(rows):
                select_row(first + j, b_ref, lists, b_list, sel.at[j])
            for j in range(rows):
                got = jnp.dot(a_ref[here + j], sel[j], preferred_element_type=jnp.float32)
                out[at * rows + j] = got.astype(out.dtype)


def product(count, groups, a, b, a_list, c_list, b_list, name, weight):
    total, block, width = a.shape
    inner, _, b_width = b.shape
    rows = total // count
    out_width = c_list.shape[0] * block
    fills = b_list.shape[0] < inner
    outs = [jax.ShapeDtypeStruct((len(group) * rows, block, out_width), a.dtype) for group in groups]
    if fills:
        outs.append(jax.ShapeDtypeStruct((2 * (inner + 8), b_width), jnp.int32))
    return pl.pallas_call(
        functools.partial(product_kernel, groups, count, fills),
        out_shape=outs,
        in_specs=[VMEM] * 5,
        out_specs=[VMEM] * len(outs),
        scratch_shapes=[pltpu.VMEM((8, 128), jnp.int32), pltpu.VMEM((rows, width, out_width), a.dtype)],
        compiler_params=pltpu.CompilerParams(vmem_limit_bytes=LIMIT),
        cost_estimate=pl.CostEstimate(flops=weight * total * block * width * out_width, bytes_accessed=0, transcendentals=0),
        name=name,
    )(a, b, a_list, c_list, b_list)


def halves_kernel(parts, a_ref, far, near):
    place = lax.axis_index("depth") // (parts // 2)
    rows = near.shape[0]
    far[...] = a_ref[pl.ds((1 - place) * rows, rows)]
    near[...] = a_ref[pl.ds(place * rows, rows)]


def halves_of(a, parts):
    half = jax.ShapeDtypeStruct((a.shape[0] // 2, *a.shape[1:]), a.dtype)
    return pl.pallas_call(
        functools.partial(halves_kernel, parts),
        out_shape=[half, half],
        in_specs=[VMEM],
        out_specs=[VMEM, VMEM],
        compiler_params=pltpu.CompilerParams(vmem_limit_bytes=LIMIT),
        cost_estimate=pl.CostEstimate(flops=0, bytes_accessed=0, transcendentals=0),
        name="halves_of_rows",
    )(a)


def after_kernel(value, earlier, out):
    out[...] = value[...]


def after(value, earlier, weight):
    return pl.pallas_call(
        after_kernel,
        out_shape=jax.ShapeDtypeStruct(value.shape, value.dtype),
        in_specs=[VMEM, VMEM],
        out_specs=VMEM,
        compiler_params=pltpu.CompilerParams(vmem_limit_bytes=LIMIT),
        cost_estimate=pl.CostEstimate(flops=weight, bytes_accessed=0, transcendentals=0),
        name="after_lists",
    )(value, earlier)


def total_of(pieces, dtype):
    return sum(one.astype(jnp.float32) for one in pieces).astype(dtype)


def sent(value, sizes, shift_row, shift_col, flip_depth):
    rows, cols, layers = sizes
    shifts = [move if isinstance(move, tuple) else (move, move) for move in (shift_row, shift_col, flip_depth)]
    pairs = []
    for r in range(rows):
        for c in range(cols):
            for l in range(layers):
                by_row, by_col, flip = (move[l % 2] for move in shifts)
                here = (r * cols + c) * layers + l
                there = (((r + by_row) % rows) * cols + (c + by_col) % cols) * layers + (l ^ flip)
                pairs.append((here, there))
    return lax.ppermute(value, AXES, pairs)


def live_columns(columns, counts, dead):
    return jnp.where(jnp.arange(columns.shape[1], dtype=jnp.int32)[:, None] < counts[None, :], columns.T, dead)


def local(sizes, a_blocks, a_columns, a_counts, b_blocks, b_columns, b_counts, c_columns, c_counts):
    layers = sizes[2]
    a, b = a_blocks[0, 0, 0], b_blocks[0, 0, 0]
    rows = a.shape[0] // layers
    evens, odds = tuple(range(0, layers, 2)), tuple(range(1, layers, 2))

    half = layers // 2
    first, second = halves_of(a, layers)
    far_first = sent(first, sizes, -1, 1, 0)
    first, a_counts, c_list = lax.optimization_barrier((first, a_counts, c_columns[0, 0].T))
    a_list = live_columns(a_columns[0, 0, 0], a_counts[0, 0, 0], b.shape[0])
    far_a_list = sent(a_list, sizes, -1, 1, 0)
    far_c_list = sent(c_list, sizes, 0, 1, 0)
    far_second = sent(after(second, a_list, GATE), sizes, -1, 1, 0)

    def paired(passed, kept):
        met = sent(passed, sizes, 0, 0, 1)
        return [total_of((one, met[at * rows : (at + 1) * rows]), a.dtype) for at, one in enumerate(kept)]

    def far_product(part, order, far_a_list, b_list):
        order_odds, order_evens = tuple(n for n in order if n % 2), tuple((n,) for n in order if n % 2 == 0)
        passed, *filled = product(half, (order_odds,), part, b, far_a_list, far_c_list, b_list, "far_passed", FAR)
        b_list = filled[0] if filled else b_list
        part, passed = lax.optimization_barrier((part, passed))
        return paired(passed, product(half, order_evens, part, b, far_a_list, far_c_list, b_list, "far_kept", FAR)), b_list

    b_live = live_columns(b_columns[0, 0, 0], b_counts[0, 0, 0], DEAD_B)
    passed, *kept, _ = product(layers, (odds,) + tuple((n,) for n in evens), a, b, a_list, c_list, b_live, "own_product", OWN)
    own = paired(passed, kept)
    far_first, passed = lax.optimization_barrier((far_first, passed))
    far, b_list = far_product(far_first, range(half, layers), far_a_list, b_live)
    far_a_list = after(far_a_list, far[-1], TURN)
    far_second, own, far_a_list = lax.optimization_barrier((far_second, own, far_a_list))
    far = far_product(far_second, range(half), far_a_list, b_list)[0] + far
    even = lax.axis_index("depth") % 2 == 0
    pieces = [own[0]] + [sent(one, sizes, 0, -1, n) for one, n in zip(far[len(evens) // 2 :], evens[len(evens) // 2 :])]
    for own_piece, own_n, far_piece, far_n in zip(own[1:], evens[1:], far, evens):
        for own_side in (0, 1):
            moves = ((0, 0, own_n), (0, -1, far_n)) if own_side == 0 else ((0, -1, far_n), (0, 0, own_n))
            mixed = jnp.where(even == (own_side == 0), own_piece, far_piece)
            pieces.append(sent(mixed, sizes, *zip(*moves)))
    counts = lax.dynamic_slice_in_dim(c_counts[0, 0], lax.axis_index("depth") * rows, rows, 0)
    slot = jnp.arange(c_list.shape[0] * b.shape[1], dtype=jnp.int32) // b.shape[1]
    live = slot[None, None, :] < counts[:, None, None]
    return jnp.where(live, total_of(pieces, jnp.float32), 0).astype(a.dtype)[None, None]


def solution(mesh):
    placed = (
        P("row", "col", "depth", None, None, None),
        P("row", "col", "depth", None, None),
        P("row", "col", "depth", None),
        P("row", "col", "depth", None, None, None),
        P("row", "col", "depth", None, None),
        P("row", "col", "depth", None),
        P("row", "col", None, None),
        P("row", "col", None),
    )
    sizes = tuple(mesh.shape[axis] for axis in AXES)
    return jax.shard_map(
        functools.partial(local, sizes),
        mesh=mesh,
        in_specs=placed,
        out_specs=P("row", "col", "depth", None, None),
        check_vma=False,
    )
```

```python
import functools

import jax
import jax.numpy as jnp
from jax import lax
from jax.experimental import pallas as pl
from jax.experimental.pallas import tpu as pltpu
from jax.sharding import PartitionSpec as P

ANY = pl.BlockSpec(memory_space=pl.ANY)
HBM = pl.BlockSpec(memory_space=pltpu.HBM)
VMEM = pl.BlockSpec(memory_space=pltpu.VMEM)
DEAD_B = -1
OWN = 2
GATE = 5 << 30
TURN = 5 << 30
LIMIT = 8 << 20
FAR = 100
AXES = ("row", "col", "depth")


def fill_b_list(b_list, live, block):
    slots, inner = live.shape
    width = b_list.shape[1]
    columns = jnp.concatenate([live[...], jnp.full((8 - slots, inner), DEAD_B, jnp.int32)]).T
    first, second = (jnp.broadcast_to(columns[:, slot : slot + 1], (inner, width)) for slot in range(2))
    left = lax.broadcasted_iota(jnp.int32, (inner, width), 1) < block
    half = b_list.shape[0] // 2
    b_list[:inner, :] = jnp.where(left, first, second)
    b_list[half : half + inner, :] = jnp.where(left, second, first)
    for start in (inner, half + inner):
        b_list[start : start + half - inner, :] = jnp.full((half - inner, width), DEAD_B, jnp.int32)


def select_row(i, b_ref, lists, b_list, sel_ref):
    inner, block, width = b_ref.shape
    a_slots, c_slots = sel_ref.shape[0] // block, sel_ref.shape[1] // block
    left = lax.broadcasted_iota(jnp.int32, (1, width), 1) < block
    listed = pltpu.roll(lists[...], lists.shape[1] - i, 1)
    target = [listed[a_slots + m, 0] for m in range(c_slots)]
    pairs = [jnp.where(left, target[m], target[m + 1]) for m in range(0, c_slots, 2)]
    for a in range(a_slots):
        k = listed[a, 0]
        straight = b_list[pl.ds(k, 1), :]
        crossed = b_list[pl.ds(k + b_list.shape[0] // 2, 1), :]
        rows = b_ref[jnp.minimum(k, inner - 1)]
        swapped = jnp.concatenate([rows[:, block:], rows[:, :block]], axis=1)
        for p, wanted in enumerate(pairs):
            keep = (straight == wanted).astype(jnp.float32).astype(rows.dtype)
            swap = (crossed == wanted).astype(jnp.float32).astype(rows.dtype)
            sel_ref[a * block : (a + 1) * block, p * width : (p + 1) * width] = rows * keep + swapped * swap


def product_kernel(groups, count, fills, *refs):
    a_ref, b_ref, a_list, c_list, b_list, *outs, lists, sel = refs
    if fills:
        live, b_list = b_list, outs.pop()
        fill_b_list(b_list, live, b_ref.shape[1])
    a_slots, listed = a_list.shape
    lists[:a_slots, :listed] = a_list[...]
    lists[a_slots : a_slots + c_list.shape[0], :listed] = c_list[...]
    me = lax.axis_index("depth")
    rows = sel.shape[0]
    for group, out in zip(groups, outs):
        for at, n in enumerate(group):
            slot = me ^ n
            first, here = slot * rows, slot % count * rows
            for j in range(rows):
                select_row(first + j, b_ref, lists, b_list, sel.at[j])
            for j in range(rows):
                got = jnp.dot(a_ref[here + j], sel[j], preferred_element_type=jnp.float32)
                out[at * rows + j] = got.astype(out.dtype)


def product(count, groups, a, b, a_list, c_list, b_list, name, weight):
    total, block, width = a.shape
    inner, _, b_width = b.shape
    rows = total // count
    out_width = c_list.shape[0] * block
    fills = b_list.shape[0] < inner
    outs = [jax.ShapeDtypeStruct((len(group) * rows, block, out_width), a.dtype) for group in groups]
    if fills:
        outs.append(jax.ShapeDtypeStruct((2 * (inner + 8), b_width), jnp.int32))
    return pl.pallas_call(
        functools.partial(product_kernel, groups, count, fills),
        out_shape=outs,
        in_specs=[VMEM] * 5,
        out_specs=[VMEM] * len(outs),
        scratch_shapes=[pltpu.VMEM((8, 128), jnp.int32), pltpu.VMEM((rows, width, out_width), a.dtype)],
        compiler_params=pltpu.CompilerParams(vmem_limit_bytes=LIMIT),
        cost_estimate=pl.CostEstimate(flops=weight * total * block * width * out_width, bytes_accessed=0, transcendentals=0),
        name=name,
    )(a, b, a_list, c_list, b_list)


def halves_kernel(parts, a_ref, far, near):
    place = lax.axis_index("depth") // (parts // 2)
    rows = near.shape[0]
    far[...] = a_ref[pl.ds((1 - place) * rows, rows)]
    near[...] = a_ref[pl.ds(place * rows, rows)]


def halves_of(a, parts):
    half = jax.ShapeDtypeStruct((a.shape[0] // 2, *a.shape[1:]), a.dtype)
    return pl.pallas_call(
        functools.partial(halves_kernel, parts),
        out_shape=[half, half],
        in_specs=[VMEM],
        out_specs=[VMEM, VMEM],
        compiler_params=pltpu.CompilerParams(vmem_limit_bytes=LIMIT),
        cost_estimate=pl.CostEstimate(flops=0, bytes_accessed=0, transcendentals=0),
        name="halves_of_rows",
    )(a)


def after_kernel(value, earlier, out):
    out[...] = value[...]


def after(value, earlier, weight):
    return pl.pallas_call(
        after_kernel,
        out_shape=jax.ShapeDtypeStruct(value.shape, value.dtype),
        in_specs=[VMEM, VMEM],
        out_specs=VMEM,
        compiler_params=pltpu.CompilerParams(vmem_limit_bytes=LIMIT),
        cost_estimate=pl.CostEstimate(flops=weight, bytes_accessed=0, transcendentals=0),
        name="after_lists",
    )(value, earlier)


def total_of(pieces, dtype):
    return sum(one.astype(jnp.float32) for one in pieces).astype(dtype)


def sent(value, sizes, shift_row, shift_col, flip_depth):
    rows, cols, layers = sizes
    shifts = [move if isinstance(move, tuple) else (move, move) for move in (shift_row, shift_col, flip_depth)]
    pairs = []
    for r in range(rows):
        for c in range(cols):
            for l in range(layers):
                by_row, by_col, flip = (move[l % 2] for move in shifts)
                here = (r * cols + c) * layers + l
                there = (((r + by_row) % rows) * cols + (c + by_col) % cols) * layers + (l ^ flip)
                pairs.append((here, there))
    return lax.ppermute(value, AXES, pairs)


def live_columns(columns, counts, dead):
    return jnp.where(jnp.arange(columns.shape[1], dtype=jnp.int32)[:, None] < counts[None, :], columns.T, dead)


def local(sizes, a_blocks, a_columns, a_counts, b_blocks, b_columns, b_counts, c_columns, c_counts):
    layers = sizes[2]
    a, b = a_blocks[0, 0, 0], b_blocks[0, 0, 0]
    rows = a.shape[0] // layers
    evens, odds = tuple(range(0, layers, 2)), tuple(range(1, layers, 2))

    half = layers // 2
    first, second = halves_of(a, layers)
    far_first = sent(first, sizes, -1, 1, 0)
    first, a_counts, c_list = lax.optimization_barrier((first, a_counts, c_columns[0, 0].T))
    a_list = live_columns(a_columns[0, 0, 0], a_counts[0, 0, 0], b.shape[0])
    far_a_list = sent(a_list, sizes, -1, 1, 0)
    far_c_list = sent(c_list, sizes, 0, 1, 0)
    far_second = sent(after(second, a_list, GATE), sizes, -1, 1, 0)

    def paired(passed, kept):
        met = sent(passed, sizes, 0, 0, 1)
        return [total_of((one, met[at * rows : (at + 1) * rows]), a.dtype) for at, one in enumerate(kept)]

    def far_product(part, order, far_a_list, b_list):
        order_odds, order_evens = tuple(n for n in order if n % 2), tuple((n,) for n in order if n % 2 == 0)
        passed, *filled = product(half, (order_odds,), part, b, far_a_list, far_c_list, b_list, "far_passed", FAR)
        b_list = filled[0] if filled else b_list
        part, passed = lax.optimization_barrier((part, passed))
        return paired(passed, product(half, order_evens, part, b, far_a_list, far_c_list, b_list, "far_kept", FAR)), b_list

    b_live = live_columns(b_columns[0, 0, 0], b_counts[0, 0, 0], DEAD_B)
    passed, *kept, _ = product(layers, (odds,) + tuple((n,) for n in evens), a, b, a_list, c_list, b_live, "own_product", OWN)
    own = paired(passed, kept)
    far_first, passed = lax.optimization_barrier((far_first, passed))
    far, b_list = far_product(far_first, range(half, layers), far_a_list, b_live)
    far_a_list = after(far_a_list, far[-1], TURN)
    far_second, own, far_a_list = lax.optimization_barrier((far_second, own, far_a_list))
    far = far_product(far_second, range(half), far_a_list, b_list)[0] + far
    pieces = [own[0]] + [sent(one, sizes, 0, 0, n) for one, n in zip(own[1:], evens[1:])]
    pieces += [sent(one, sizes, 0, -1, n) for one, n in zip(far, evens)]
    counts = lax.dynamic_slice_in_dim(c_counts[0, 0], lax.axis_index("depth") * rows, rows, 0)
    slot = jnp.arange(c_list.shape[0] * b.shape[1], dtype=jnp.int32) // b.shape[1]
    live = slot[None, None, :] < counts[:, None, None]
    return jnp.where(live, total_of(pieces, jnp.float32), 0).astype(a.dtype)[None, None]


def solution(mesh):
    placed = (
        P("row", "col", "depth", None, None, None),
        P("row", "col", "depth", None, None),
        P("row", "col", "depth", None),
        P("row", "col", "depth", None, None, None),
        P("row", "col", "depth", None, None),
        P("row", "col", "depth", None),
        P("row", "col", None, None),
        P("row", "col", None),
    )
    sizes = tuple(mesh.shape[axis] for axis in AXES)
    return jax.shard_map(
        functools.partial(local, sizes),
        mesh=mesh,
        in_specs=placed,
        out_specs=P("row", "col", "depth", None, None),
        check_vma=False,
    )
```
